32 devices in a mesh: crop: 4 (over x, core), seq: 8 (over z, y).
Axes of the slice: x: 2, y: 2, z: 4, core: 2. Of those that a mesh axis runs over, the one named last changes fastest.
Arguments:
- queries: bfloat16 [4096, 2048], P(('crop', 'seq')), parts along dimension 0, may hold values from -13 to 13
- keys: bfloat16 [4096, 2048], P(('crop', 'seq')), parts along dimension 0, may hold values from -6 to 6
- values: bfloat16 [4096, 2048], P(('crop', 'seq')), parts along dimension 0, may hold values from -6 to 6
- proj_weight: bfloat16 [2048, 256], replicated, may hold values from -0.125 to 0.125
- norm_gain: float32 [256], replicated, may hold values from 0.1 to 1.9
- conv_weight: bfloat16 [9, 256, 256], replicated, may hold values from -0.125 to 0.125
- conv_bias: float32 [256], replicated, may hold values from -3 to 3
- class_weight: bfloat16 [9, 16, 256], replicated, may hold values from -4.5 to 4.5
- class_bias: float32 [16], replicated, may hold values from -4 to 4
- labels: int32 [256, 256], P(('crop', 'seq')), parts along dimension 0, may hold values from 0 to 15
Outputs:
- logits: float32 [16, 256, 256], P(None, ('crop', 'seq')), parts along dimension 1
- pixel_loss: float32 [256, 256], P(('crop', 'seq')), parts along dimension 0
- loss: float32 [4], P('crop'), parts along dimension 0
The draws below stay inside these ranges and needn't reach their ends.
There are 4 independent parts, one for each index of `crop`. The reference program is written for one: setup_inputs(seed, part) draws one part's arguments, and reference() takes and returns one part's arrays. A program takes and returns all parts, laid end to end along the dimension named above; an argument that names none is the same for every part. Nothing has to cross between parts.
All inputs are finite; a program needn't handle non-finite values.
Results may differ from the reference program's by a relative error of at most 0.0085.
The reference program's roundings to bfloat16 on the way count: a program that leaves them out, or rounds other values in their place, can miss the bound.
Values may be sent and summed in bfloat16 or wider, within the bound.
A program may use at most 64 MiB of HBM per device.

```python
import math
import jax
import jax.numpy as jnp
from jax import lax

HEADS = 16
HEAD_DIM = 128
CHANNELS = 256
CLASSES = 16
UPSCALE = 4
GRID_COLS = 64
GRID_ROWS = 16
TOKENS = 1024
PIX_ROWS = 64
PIX_COLS = 256


def paired_draw(key):
    shape = (TOKENS, HEADS * HEAD_DIM)
    key_base = jnp.clip(jax.random.normal(jax.random.fold_in(key, 11), shape, jnp.float32), -6.0, 6.0)
    query_base = jnp.clip(jax.random.normal(jax.random.fold_in(key, 12), shape, jnp.float32), -6.0, 6.0)
    return (query_base, key_base)


def draw_queries(key, part):
    return paired_draw(key)[0].astype(jnp.bfloat16)


def draw_keys(key, part):
    return paired_draw(key)[1].astype(jnp.bfloat16)


def draw_class_weight(key, part):
    shape = (9, CLASSES, CHANNELS)
    spread = 2.0 * CHANNELS ** (-0.5)
    drawn = jnp.clip(jax.random.normal(jax.random.fold_in(key, 34), shape, jnp.float32), -6.0, 6.0) * spread
    return drawn.astype(jnp.bfloat16)


def plant(values, key, smallest, top_value):
    extent = values.shape
    place = [jax.random.randint(jax.random.fold_in(key, axis), (), 0, extent[axis]) for axis in range(len(extent))]
    values = values.at[tuple(place)].set(smallest)
    longest = extent.index(max(extent))
    place[longest] = (place[longest] + 1) % extent[longest]
    return values.at[tuple(place)].set(top_value)


def block_levels(own_key, shape, split, smallest, top_value):
    def one(position, shards_of):
        draws = jax.random.uniform(jax.random.fold_in(jax.random.fold_in(own_key, 6), position), (shards_of,), jnp.float32, smallest / len(split), top_value / len(split))
        return jnp.repeat(jnp.exp(draws), shape[position] // shards_of).reshape((-1,) + (1,) * (len(shape) - position - 1))

    factor_of = one(*split[0])
    for cut in split[1:]:
        factor_of = factor_of * one(*cut)
    return factor_of


def noise(stream_key, extent, width, bound, shards=(), kind=jnp.bfloat16):
    entries = jax.random.normal(stream_key, extent, jnp.float32) * width
    if len(shards) > 0:
        entries = block_levels(stream_key, extent, shards, -0.22, 0.18) * entries
    return jnp.clip(entries, min=-bound, max=bound).astype(kind)


def setup_inputs(seed: int = 0, part: int = 0) -> dict:
    key_of = jax.random.split(jax.random.key(seed), 11)
    part_keys = jax.random.split(jax.random.fold_in(key_of[10], part), 11)
    return {
        "queries": draw_queries(jax.random.fold_in(jax.random.fold_in(key_of[10], part), 71), part),
        "keys": draw_keys(jax.random.fold_in(jax.random.fold_in(key_of[10], part), 71), part),
        "values": noise(part_keys[2], (TOKENS, HEADS * HEAD_DIM), 1.0, 6.0, ((0, 8),)),
        "proj_weight": noise(key_of[3], (HEADS * HEAD_DIM, CHANNELS), (HEADS * HEAD_DIM) ** -0.5, 0.125),
        "norm_gain": jnp.clip(1.0 + 0.18 * jax.random.normal(key_of[4], (CHANNELS,), jnp.float32), 0.1, 1.9),
        "conv_weight": noise(key_of[5], (9, CHANNELS, CHANNELS), (9 * CHANNELS) ** -0.5, 0.125),
        "conv_bias": noise(key_of[6], (CHANNELS,), 0.5, 3.0, (), jnp.float32),
        "class_weight": draw_class_weight(jax.random.fold_in(key_of[10], 71), part),
        "class_bias": noise(key_of[8], (CLASSES,), 1.0, 4.0, (), jnp.float32),
        "labels": plant(jax.random.randint(part_keys[9], (PIX_ROWS, PIX_COLS), 0, CLASSES), jax.random.fold_in(part_keys[9], 1), 0, CLASSES - 1).astype(jnp.int32),
    }


EPSILON = 1e-05

def rotate(packed, row_ids, col_ids):
    count_rows = packed.shape[0]
    head_rows = packed.reshape(count_rows, HEADS, HEAD_DIM).astype(jnp.float32)
    quarter = HEAD_DIM // 4
    omegas = jnp.power(jnp.float32(100.0), -jnp.arange(quarter, dtype=jnp.float32) / quarter)
    pieces = []
    for coords, offset in ((row_ids, 0), (col_ids, 2 * quarter)):
        angles = coords.astype(jnp.float32)[:, None, None] * omegas[None, None, :]
        cosine = jnp.cos(angles)
        sine_part = jnp.sin(angles)
        first_half = head_rows[:, :, offset:offset + quarter]
        second_half = head_rows[:, :, offset + quarter:offset + 2 * quarter]
        pieces.append(first_half * cosine - second_half * sine_part)
        pieces.append(second_half * cosine + first_half * sine_part)
    return jnp.concatenate(pieces, axis=2).reshape(count_rows, HEADS * HEAD_DIM).astype(jnp.bfloat16)

def attend(queries, keys, values):
    total_rows = queries.shape[0]
    block = math.gcd(512, total_rows)
    scale = queries.shape[2] ** (-0.5)
    keys_wide = keys.astype(jnp.float32)
    values_wide = values.astype(jnp.float32)

    def one_block(query_block):
        scores = jnp.einsum('qhd,khd->hqk', query_block.astype(jnp.float32), keys_wide) * scale
        highest = lax.optimization_barrier(jnp.max(scores, axis=2, keepdims=True))
        exponent = jnp.exp(scores - highest)
        weights = (exponent / lax.optimization_barrier(jnp.sum(exponent, axis=2, keepdims=True))).astype(jnp.bfloat16)
        mixed = jnp.einsum('hqk,khd->qhd', weights.astype(jnp.float32), values_wide)
        return mixed.astype(jnp.bfloat16)
    blocked = queries.reshape(total_rows // block, block, queries.shape[1], queries.shape[2])
    return lax.map(one_block, blocked).reshape(queries.shape)

def normalize(features, gain):
    center = lax.optimization_barrier(jnp.mean(features, axis=-1, keepdims=True))
    spread = lax.optimization_barrier(jnp.mean((features - center) ** 2, axis=-1, keepdims=True))
    return (features - center) / jnp.sqrt(spread + EPSILON) * gain

def convolve(padded, weight):
    out_rows = padded.shape[0] - 2
    out_cols = padded.shape[1] - 2
    summed = jnp.zeros((out_rows * out_cols, weight.shape[2]), jnp.float32)
    for tap_index in range(9):
        tap_row, tap_col = (tap_index // 3, tap_index % 3)
        window = padded[tap_row:tap_row + out_rows, tap_col:tap_col + out_cols].reshape(-1, padded.shape[2])
        summed = summed + jnp.dot(window, weight[tap_index], preferred_element_type=jnp.float32)
    return summed.reshape(out_rows, out_cols, weight.shape[2])

def classify(padded, class_weight):
    out_rows = padded.shape[0] - 2
    out_cols = padded.shape[1] - 2
    summed = jnp.zeros((class_weight.shape[1], out_rows * out_cols), jnp.float32)
    for tap_index in range(9):
        tap_row, tap_col = (tap_index // 3, tap_index % 3)
        window = padded[tap_row:tap_row + out_rows, tap_col:tap_col + out_cols].reshape(-1, padded.shape[2])
        summed = summed + lax.dot_general(class_weight[tap_index], window, (((1,), (1,)), ((), ())), preferred_element_type=jnp.float32)
    return summed.reshape(class_weight.shape[1], out_rows, out_cols)

def pixel_losses(logits, labels):
    highest = lax.optimization_barrier(jnp.max(logits, axis=0))
    log_total = highest + jnp.log(lax.optimization_barrier(jnp.sum(jnp.exp(logits - highest[None]), axis=0)))
    class_ids = jnp.arange(logits.shape[0], dtype=jnp.int32)[:, None, None]
    picked = lax.optimization_barrier(jnp.sum(jnp.where(class_ids == labels[None], logits, jnp.zeros_like(logits)), axis=0))
    return log_total - picked

def reference(queries, keys, values, proj_weight, norm_gain, conv_weight, conv_bias, class_weight, class_bias, labels):
    positions = jnp.arange(TOKENS, dtype=jnp.int32)
    row_ids = positions // GRID_COLS
    col_ids = positions % GRID_COLS
    rotated_queries = rotate(queries, row_ids, col_ids).reshape(TOKENS, HEADS, HEAD_DIM)
    rotated_keys = rotate(keys, row_ids, col_ids).reshape(TOKENS, HEADS, HEAD_DIM)
    mixed = attend(rotated_queries, rotated_keys, values.reshape(TOKENS, HEADS, HEAD_DIM))
    mixed = mixed.reshape(TOKENS, HEADS * HEAD_DIM)
    features = jnp.dot(mixed, proj_weight, preferred_element_type=jnp.float32)
    activated = jax.nn.gelu(normalize(features, norm_gain), approximate=False).astype(jnp.bfloat16)
    activated = activated.reshape(GRID_ROWS, GRID_COLS, -1)
    padded = jnp.pad(activated, ((1, 1), (1, 1), (0, 0)))
    hidden = jax.nn.gelu(convolve(padded, conv_weight) + conv_bias, approximate=False).astype(jnp.bfloat16)
    upsampled = jnp.repeat(jnp.repeat(hidden, UPSCALE, axis=0), UPSCALE, axis=1)
    logits = classify(jnp.pad(upsampled, ((1, 1), (1, 1), (0, 0))), class_weight) + class_bias[:, None, None]
    losses = pixel_losses(logits, labels)
    loss = (jnp.sum(losses) / (PIX_ROWS * PIX_COLS)).reshape(1)
    return (logits, losses, loss)
```

```python
import functools
import math

import jax
import jax.numpy as jnp
import numpy as np
from jax import lax
from jax.experimental import pallas as pl
from jax.experimental.pallas import tpu as pltpu
from jax.sharding import PartitionSpec as P

HEADS = 16
HEAD_DIM = 128
UPSCALE = 4
GRID_COLS = 64
EPSILON = 1e-05
MESH = pl.DeviceIdType.MESH
F32 = jnp.float32
BF16 = jnp.bfloat16


def gelu(x):
    return 0.5 * x * (1.0 + lax.erf(x * (2.0**-0.5)))


def tables(grid_rows):
    quarter = HEAD_DIM // 4
    omegas = np.power(np.float32(100.0), -np.arange(quarter, dtype=np.float32) / quarter)

    def half(count, offset):
        angles = np.arange(count, dtype=np.float32)[:, None] * omegas[None, :].astype(np.float32)
        cosine = np.cos(angles.astype(np.float64)).astype(np.float32)
        sine = np.sin(angles.astype(np.float64)).astype(np.float32)
        out = np.zeros((3, count, HEAD_DIM), np.float32)
        out[0, :, offset : offset + quarter] = cosine
        out[0, :, offset + quarter : offset + 2 * quarter] = cosine
        out[1, :, offset : offset + quarter] = -sine
        out[2, :, offset + quarter : offset + 2 * quarter] = sine
        return out

    return half(grid_rows, 0), half(GRID_COLS, 2 * quarter)


def kernel(
    n,
    q_ref,
    k_ref,
    v_ref,
    pw_ref,
    gain_ref,
    cw_ref,
    cb_ref,
    tw_ref,
    tb_ref,
    lab_ref,
    row_ref,
    col_ref,
    up_ref,
    logits_ref,
    losses_ref,
    loss_ref,
    qx,
    kx,
    pw,
    cw,
    rq,
    rk,
    qbuf,
    kbuf,
    vbuf,
    obuf,
    mix,
    ext,
    part_sum,
    sums,
    ssem,
    rsem,
    osend,
    orecv,
    hsend,
    hrecv,
    lsend,
    lrecv,
    local,
):
    me = lax.axis_index("seq")
    hpd, keys, dim = kbuf.shape
    tokens = keys // n
    part = qbuf.shape[1] // n
    split = tokens // part
    strip = tokens // GRID_COLS
    my_group = me // split
    my_part = lax.rem(me, split)

    def peer(i):
        off = n // 2 + ((i + 1) // 2) * (1 - 2 * lax.rem(i, 2))
        return lax.rem(me + off, n)

    def each_peer(fn):
        def step(i, carry):
            fn(peer(i))
            return carry

        lax.fori_loop(0, n - 1, step, 0)

    barrier = pltpu.get_barrier_semaphore()
    each_peer(
        lambda d: pl.semaphore_signal(barrier, inc=1, device_id={"seq": d}, device_id_type=MESH)
    )
    load_k = pltpu.make_async_copy(k_ref, kx, local.at[0])
    load_q = pltpu.make_async_copy(q_ref, qx, local.at[1])
    load_pw = pltpu.make_async_copy(pw_ref, pw, local.at[2])
    load_cw = pltpu.make_async_copy(cw_ref, cw, local.at[3])
    load_k.start()
    load_q.start()
    own_v = []
    for h in range(hpd):
        cols = pl.ds(pl.multiple_of((my_group * hpd + h) * dim, dim), dim)
        rows = pl.ds(pl.multiple_of(me * tokens, tokens), tokens)
        copy = pltpu.make_async_copy(v_ref.at[:, cols], vbuf.at[h, rows], local.at[4 + h])
        copy.start()
        own_v.append(copy)
    load_pw.start()
    load_cw.start()

    turn = []
    for t in range(3):
        pieces = []
        for r in range(strip):
            pieces.append(row_ref[t, pl.ds(me * strip + r, 1), :] + col_ref[t])
        turn.append(jnp.concatenate(pieces, axis=0) if strip > 1 else pieces[0])

    def rotate(src, dst, h):
        for g in range(HEADS // hpd):
            head = g * hpd + h
            x = src[:, head * dim : (head + 1) * dim].astype(F32)
            out = x * turn[0] + pltpu.roll(x, 96, 1) * turn[1] + pltpu.roll(x, 32, 1) * turn[2]
            dst[head] = out.astype(BF16)

    def v_copy(h, d, s):
        head = (d // split) * hpd + h
        return pltpu.make_async_remote_copy(
            src_ref=v_ref.at[:, pl.ds(pl.multiple_of(head * dim, dim), dim)],
            dst_ref=vbuf.at[h, pl.ds(pl.multiple_of(s * tokens, tokens), tokens)],
            send_sem=ssem.at[0, h, d],
            recv_sem=rsem.at[0, h, s],
            device_id={"seq": d},
            device_id_type=MESH,
        )

    def k_copy(h, d, s):
        return pltpu.make_async_remote_copy(
            src_ref=rk.at[(d // split) * hpd + h],
            dst_ref=kbuf.at[h, pl.ds(pl.multiple_of(s * tokens, tokens), tokens)],
            send_sem=ssem.at[1, h, d],
            recv_sem=rsem.at[1, h, s],
            device_id={"seq": d},
            device_id_type=MESH,
        )

    def q_copy(h, d, s):
        rows = pl.ds(pl.multiple_of(lax.rem(d, split) * part, part), part)
        return pltpu.make_async_remote_copy(
            src_ref=rq.at[(d // split) * hpd + h, rows],
            dst_ref=qbuf.at[h, pl.ds(pl.multiple_of(s * part, part), part)],
            send_sem=ssem.at[2, h, d],
            recv_sem=rsem.at[2, h, s],
            device_id={"seq": d},
            device_id_type=MESH,
        )

    load_k.wait()
    rotate(kx, rk, 0)
    pl.semaphore_wait(barrier, n - 1)
    for h in range(hpd):
        if h > 0:
            rotate(kx, rk, h)
        each_peer(lambda d: k_copy(h, d, me).start())
        if h == 0:
            load_q.wait()
        rotate(qx, rq, h)
        each_peer(lambda d: q_copy(h, d, me).start())
        each_peer(lambda d: v_copy(h, d, me).start())
        head = my_group * hpd + h
        kbuf[h, pl.ds(pl.multiple_of(me * tokens, tokens), tokens), :] = rk[head]
        qbuf[h, pl.ds(pl.multiple_of(me * part, part), part), :] = rq[
            head, pl.ds(pl.multiple_of(my_part * part, part), part), :
        ]

    def o_copy(h, d, s):
        head = (s // split) * hpd + h
        return pltpu.make_async_remote_copy(
            src_ref=obuf.at[h, pl.ds(pl.multiple_of(d * part, part), part)],
            dst_ref=mix.at[
                pl.ds(pl.multiple_of(lax.rem(s, split) * part, part), part),
                pl.ds(pl.multiple_of(head * dim, dim), dim),
            ],
            send_sem=osend.at[h, d],
            recv_sem=orecv.at[h, s],
            device_id={"seq": d},
            device_id_type=MESH,
        )

    block = min(256, n * part)
    in_block = block // part
    blocks = n * part // block
    factor = dim ** (-0.5) * math.log2(math.e)

    for h in range(hpd):
        each_peer(lambda s: k_copy(h, s, s).wait_recv())
        each_peer(lambda s: q_copy(h, s, s).wait_recv())
        own_v[h].wait()
        each_peer(lambda s: v_copy(h, s, s).wait_recv())

        def attend(i, carry):
            j = lax.rem(me // in_block + blocks // 2 + i, blocks)
            rows = pl.ds(pl.multiple_of(j * block, block), block)
            scores = lax.dot_general(
                qbuf[h, rows, :], kbuf[h], (((1,), (1,)), ((), ())), preferred_element_type=F32
            )
            highest = jnp.max(scores, axis=1, keepdims=True)
            exponent = jnp.exp2((scores - highest) * factor)
            total = jnp.sum(exponent, axis=1, keepdims=True)
            weights = (exponent * (1.0 / total)).astype(BF16)
            mixed = jnp.dot(weights, vbuf[h], preferred_element_type=F32)
            obuf[h, rows, :] = mixed.astype(BF16)
            for u in range(in_block):
                d = j * in_block + u

                @pl.when(d != me)
                def _():
                    o_copy(h, d, me).start()

            return carry

        lax.fori_loop(0, blocks, attend, 0, unroll=blocks <= 4)
        head = my_group * hpd + h
        mix[
            pl.ds(pl.multiple_of(my_part * part, part), part),
            pl.ds(pl.multiple_of(head * dim, dim), dim),
        ] = obuf[h, pl.ds(pl.multiple_of(me * part, part), part), :]

    load_pw.wait()
    for h in range(hpd):
        each_peer(lambda s: o_copy(h, s, s).wait_recv())
    features = jnp.dot(mix[...], pw[...], preferred_element_type=F32)
    center = jnp.mean(features, axis=-1, keepdims=True)
    shifted = features - center
    spread = jnp.mean(shifted * shifted, axis=-1, keepdims=True)
    act = gelu(shifted / jnp.sqrt(spread + EPSILON) * gain_ref[...]).astype(BF16)
    cols = GRID_COLS
    halo = 2 * cols
    ext[halo : halo + tokens, :] = act

    up, down = lax.rem(me + 1, n), lax.rem(me + n - 1, n)
    to_up = pltpu.make_async_remote_copy(
        src_ref=ext.at[tokens : tokens + halo],
        dst_ref=ext.at[0:halo],
        send_sem=hsend.at[0],
        recv_sem=hrecv.at[0],
        device_id={"seq": up},
        device_id_type=MESH,
    )
    to_down = pltpu.make_async_remote_copy(
        src_ref=ext.at[halo : 2 * halo],
        dst_ref=ext.at[halo + tokens : 2 * halo + tokens],
        send_sem=hsend.at[1],
        recv_sem=hrecv.at[1],
        device_id={"seq": down},
        device_id_type=MESH,
    )
    to_up.start()
    to_down.start()
    load_cw.wait()
    to_up.wait()
    to_down.wait()

    place = lax.broadcasted_iota(jnp.int32, (tokens + 2 * halo, 1), 0)
    grid_row = place // cols + (me * strip - 2)
    inside = (grid_row >= 0) & (grid_row < strip * n)
    window = jnp.where(inside, ext[...].astype(F32), 0.0).astype(BF16)
    count = tokens + 2 * cols
    by_col = []
    for s in range(3):
        summed = None
        for r in range(3):
            term = jnp.dot(
                window[r * cols : r * cols + count], cw[3 * r + s], preferred_element_type=F32
            )
            summed = term if summed is None else summed + term
        by_col.append(summed)
    column = lax.rem(lax.broadcasted_iota(jnp.int32, (count, 1), 0), cols)
    conv = (
        by_col[1]
        + jnp.where(column == 0, 0.0, pltpu.roll(by_col[0], 1, 0))
        + jnp.where(column == cols - 1, 0.0, pltpu.roll(by_col[2], count - 1, 0))
    )
    hidden = jnp.where(inside[cols : cols + count], gelu(conv + cb_ref[...]), 0.0).astype(BF16)

    width = cols * UPSCALE
    lane = lax.broadcasted_iota(jnp.int32, (1, width), 1)
    classes = tb_ref.shape[0]
    rows_of = []
    for r in range(strip + 2):
        wide = jnp.dot(
            up_ref[...], hidden[r * cols : (r + 1) * cols], preferred_element_type=F32
        ).astype(BF16)
        taps = lax.dot_general(
            tw_ref[...], wide, (((1,), (1,)), ((), ())), preferred_element_type=F32
        )
        tap = lambda i: taps[i * classes : (i + 1) * classes]
        rows_of.append(
            [
                tap(3 * t + 1)
                + jnp.where(lane == 0, 0.0, pltpu.roll(tap(3 * t), 1, 1))
                + jnp.where(lane == width - 1, 0.0, pltpu.roll(tap(3 * t + 2), width - 1, 1))
                for t in range(3)
            ]
        )
    bias = tb_ref[...]
    ids = lax.broadcasted_iota(jnp.int32, (classes, width), 0)
    running = jnp.zeros((1, width), F32)
    for r in range(strip):
        low, here, high = rows_of[r], rows_of[r + 1], rows_of[r + 2]
        inner = here[0] + here[1] + here[2] + bias
        for phase in range(UPSCALE):
            if phase == 0:
                out = low[0] + here[1] + here[2] + bias
            elif phase == UPSCALE - 1:
                out = here[0] + here[1] + high[2] + bias
            else:
                out = inner
            y = r * UPSCALE + phase
            logits_ref[:, y, :] = out
            if phase != 2:
                highest = jnp.max(out, axis=0, keepdims=True)
                lse = highest + jnp.log(jnp.sum(jnp.exp(out - highest), axis=0, keepdims=True))
            picked = jnp.sum(
                jnp.where(ids == lab_ref[y : y + 1, :], out, 0.0), axis=0, keepdims=True
            )
            lost = lse - picked
            losses_ref[y : y + 1, :] = lost
            running = running + lost

    total = jnp.sum(running, axis=1, keepdims=True)
    part_sum[...] = jnp.broadcast_to(total, part_sum.shape)

    def l_copy(d, s):
        return pltpu.make_async_remote_copy(
            src_ref=part_sum,
            dst_ref=sums.at[s],
            send_sem=lsend.at[d],
            recv_sem=lrecv.at[s],
            device_id={"seq": d},
            device_id_type=MESH,
        )

    each_peer(lambda d: l_copy(d, me).start())
    sums[me] = part_sum[...]
    for h in range(hpd):
        each_peer(lambda d: v_copy(h, d, me).wait_send())
        each_peer(lambda d: k_copy(h, d, me).wait_send())
        each_peer(lambda d: q_copy(h, d, me).wait_send())
        each_peer(lambda d: o_copy(h, d, me).wait_send())
    each_peer(lambda s: l_copy(s, s).wait_recv())
    each_peer(lambda d: l_copy(d, me).wait_send())
    pixels = n * strip * UPSCALE * width
    loss_ref[...] = jnp.sum(sums[...], axis=0)[0:1, 0:1] / pixels


def body(
    queries,
    keys,
    values,
    proj_weight,
    norm_gain,
    conv_weight,
    conv_bias,
    class_weight,
    class_bias,
    labels,
):
    n = lax.axis_size("seq")
    tokens = queries.shape[0]
    strip = tokens // GRID_COLS
    hpd = max(1, HEADS // n)
    split = max(1, n // HEADS)
    part = tokens // split
    channels = proj_weight.shape[1]
    classes = class_weight.shape[1]
    row_table, col_table = tables(strip * n)
    spread = np.zeros((GRID_COLS * UPSCALE, GRID_COLS), np.float32)
    spread[np.arange(GRID_COLS * UPSCALE), np.arange(GRID_COLS * UPSCALE) // UPSCALE] = 1.0
    hbm = pl.BlockSpec(memory_space=pl.ANY)
    vmem = pl.BlockSpec(memory_space=pltpu.VMEM)
    dma = pltpu.SemaphoreType.DMA
    logits, losses, loss = pl.pallas_call(
        functools.partial(kernel, n),
        out_shape=(
            jax.ShapeDtypeStruct((classes,) + labels.shape, F32),
            jax.ShapeDtypeStruct(labels.shape, F32),
            jax.ShapeDtypeStruct((1, 1), F32),
        ),
        in_specs=[hbm, hbm, hbm, hbm, vmem, hbm] + [vmem] * 7,
        out_specs=(vmem, vmem, vmem),
        scratch_shapes=[
            pltpu.VMEM((tokens, HEADS * HEAD_DIM), BF16),
            pltpu.VMEM((tokens, HEADS * HEAD_DIM), BF16),
            pltpu.VMEM(proj_weight.shape, BF16),
            pltpu.VMEM(conv_weight.shape, BF16),
            pltpu.VMEM((HEADS, tokens, HEAD_DIM), BF16),
            pltpu.VMEM((HEADS, tokens, HEAD_DIM), BF16),
            pltpu.VMEM((hpd, n * part, HEAD_DIM), BF16),
            pltpu.VMEM((hpd, n * tokens, HEAD_DIM), BF16),
            pltpu.VMEM((hpd, n * tokens, HEAD_DIM), BF16),
            pltpu.VMEM((hpd, n * part, HEAD_DIM), BF16),
            pltpu.VMEM((tokens, HEADS * HEAD_DIM), BF16),
            pltpu.VMEM((tokens + 4 * GRID_COLS, channels), BF16),
            pltpu.VMEM((8, 128), F32),
            pltpu.VMEM((n, 8, 128), F32),
            dma((3, hpd, n)),
            dma((3, hpd, n)),
            dma((hpd, n)),
            dma((hpd, n)),
            dma((2,)),
            dma((2,)),
            dma((n,)),
            dma((n,)),
            dma((4 + hpd,)),
        ],
        compiler_params=pltpu.CompilerParams(
            collective_id=0, has_side_effects=True, vmem_limit_bytes=56 * 1024 * 1024
        ),
    )(
        queries,
        keys,
        values,
        proj_weight,
        norm_gain.reshape(1, -1),
        conv_weight,
        conv_bias.reshape(1, -1),
        class_weight.reshape(-1, class_weight.shape[2]),
        class_bias.reshape(-1, 1),
        labels,
        jnp.asarray(row_table),
        jnp.asarray(col_table),
        jnp.asarray(spread, BF16),
    )
    return logits, losses, loss.reshape(1)


def solution(mesh):
    rows = P(("crop", "seq"), None)
    in_specs = (rows, rows, rows, P(), P(), P(), P(), P(), P(), rows)
    out_specs = (P(None, ("crop", "seq"), None), rows, P("crop"))
    return jax.shard_map(body, mesh=mesh, in_specs=in_specs, out_specs=out_specs, check_vma=False)
```

```python
import functools
import math

import jax
import jax.numpy as jnp
import numpy as np
from jax import lax
from jax.experimental import pallas as pl
from jax.experimental.pallas import tpu as pltpu
from jax.sharding import PartitionSpec as P

HEADS = 16
HEAD_DIM = 128
UPSCALE = 4
GRID_COLS = 64
EPSILON = 1e-05
MESH = pl.DeviceIdType.MESH
F32 = jnp.float32
BF16 = jnp.bfloat16


def gelu(x):
    return 0.5 * x * (1.0 + lax.erf(x * (2.0**-0.5)))


def tables(grid_rows):
    quarter = HEAD_DIM // 4
    omegas = np.power(np.float32(100.0), -np.arange(quarter, dtype=np.float32) / quarter)

    def half(count, offset):
        angles = np.arange(count, dtype=np.float32)[:, None] * omegas[None, :].astype(np.float32)
        cosine = np.cos(angles.astype(np.float64)).astype(np.float32)
        sine = np.sin(angles.astype(np.float64)).astype(np.float32)
        out = np.zeros((3, count, HEAD_DIM), np.float32)
        out[0, :, offset : offset + quarter] = cosine
        out[0, :, offset + quarter : offset + 2 * quarter] = cosine
        out[1, :, offset : offset + quarter] = -sine
        out[2, :, offset + quarter : offset + 2 * quarter] = sine
        return out

    return half(grid_rows, 0), half(GRID_COLS, 2 * quarter)


def kernel(
    n,
    q_ref,
    k_ref,
    v_ref,
    pw_ref,
    gain_in,
    cw_ref,
    cb_in,
    tw_in,
    tb_in,
    lab_in,
    row_in,
    col_in,
    up_in,
    logits_out,
    losses_out,
    loss_ref,
    gain_ref,
    cb_ref,
    tw_ref,
    tb_ref,
    lab_ref,
    row_ref,
    col_ref,
    up_ref,
    logits_ref,
    losses_ref,
    qx,
    kx,
    pw,
    cw,
    rq,
    rk,
    qbuf,
    kbuf,
    vbuf,
    obuf,
    mix,
    ext,
    part_sum,
    sums,
    ssem,
    rsem,
    osend,
    orecv,
    hsend,
    hrecv,
    lsend,
    lrecv,
    local,
    small,
    results,
):
    me = lax.axis_index("seq")
    hpd, keys, dim = kbuf.shape
    tokens = keys // n
    part = qbuf.shape[1] // n
    split = tokens // part
    strip = tokens // GRID_COLS
    my_group = me // split
    my_part = lax.rem(me, split)

    def peer(i):
        off = n // 2 + ((i + 1) // 2) * (1 - 2 * lax.rem(i, 2))
        return lax.rem(me + off, n)

    def each_peer(fn):
        def step(i, carry):
            fn(peer(i))
            return carry

        lax.fori_loop(0, n - 1, step, 0)

    def v_copy(h, d, s):
        head = (d // split) * hpd + h
        return pltpu.make_async_remote_copy(
            src_ref=v_ref.at[:, pl.ds(pl.multiple_of(head * dim, dim), dim)],
            dst_ref=vbuf.at[h, pl.ds(pl.multiple_of(s * tokens, tokens), tokens)],
            send_sem=ssem.at[0, h, d],
            recv_sem=rsem.at[0, h, s],
            device_id={"seq": d},
            device_id_type=MESH,
        )

    barrier = pltpu.get_barrier_semaphore()
    each_peer(
        lambda d: pl.semaphore_signal(barrier, inc=1, device_id={"seq": d}, device_id_type=MESH)
    )
    load_k = pltpu.make_async_copy(k_ref, kx, local.at[0])
    load_q = pltpu.make_async_copy(q_ref, qx, local.at[1])
    load_pw = pltpu.make_async_copy(pw_ref, pw, local.at[2])
    load_cw = pltpu.make_async_copy(cw_ref, cw, local.at[3])
    first = [
        pltpu.make_async_copy(a, b, small.at[i])
        for i, (a, b) in enumerate(((row_in, row_ref), (col_in, col_ref)))
    ]
    later = [
        pltpu.make_async_copy(a, b, small.at[i + 2])
        for i, (a, b) in enumerate(
            (
                (gain_in, gain_ref),
                (cb_in, cb_ref),
                (tw_in, tw_ref),
                (tb_in, tb_ref),
                (lab_in, lab_ref),
                (up_in, up_ref),
            )
        )
    ]
    load_k.start()
    for copy in first:
        copy.start()
    load_q.start()
    own_v = []
    for h in range(hpd):
        cols = pl.ds(pl.multiple_of((my_group * hpd + h) * dim, dim), dim)
        rows = pl.ds(pl.multiple_of(me * tokens, tokens), tokens)
        copy = pltpu.make_async_copy(v_ref.at[:, cols], vbuf.at[h, rows], local.at[4 + h])
        copy.start()
        own_v.append(copy)
    pl.semaphore_wait(barrier, n - 1)
    each_peer(lambda d: v_copy(0, d, me).start())
    load_pw.start()
    load_cw.start()
    for copy in later:
        copy.start()
    for copy in first:
        copy.wait()

    turn = []
    for t in range(3):
        pieces = []
        for r in range(strip):
            pieces.append(row_ref[t, pl.ds(me * strip + r, 1), :] + col_ref[t])
        turn.append(jnp.concatenate(pieces, axis=0) if strip > 1 else pieces[0])

    def rotate(src, dst, h):
        for g in range(HEADS // hpd):
            head = g * hpd + h
            x = src[:, head * dim : (head + 1) * dim].astype(F32)
            out = x * turn[0] + pltpu.roll(x, 96, 1) * turn[1] + pltpu.roll(x, 32, 1) * turn[2]
            dst[head] = out.astype(BF16)

    def k_copy(h, d, s):
        return pltpu.make_async_remote_copy(
            src_ref=rk.at[(d // split) * hpd + h],
            dst_ref=kbuf.at[h, pl.ds(pl.multiple_of(s * tokens, tokens), tokens)],
            send_sem=ssem.at[1, h, d],
            recv_sem=rsem.at[1, h, s],
            device_id={"seq": d},
            device_id_type=MESH,
        )

    def q_copy(h, d, s):
        rows = pl.ds(pl.multiple_of(lax.rem(d, split) * part, part), part)
        return pltpu.make_async_remote_copy(
            src_ref=rq.at[(d // split) * hpd + h, rows],
            dst_ref=qbuf.at[h, pl.ds(pl.multiple_of(s * part, part), part)],
            send_sem=ssem.at[2, h, d],
            recv_sem=rsem.at[2, h, s],
            device_id={"seq": d},
            device_id_type=MESH,
        )

    load_k.wait()
    for h in range(hpd):
        rotate(kx, rk, h)
        each_peer(lambda d: k_copy(h, d, me).start())
        if h == 0:
            load_q.wait()
        rotate(qx, rq, h)
        each_peer(lambda d: q_copy(h, d, me).start())
        if h + 1 < hpd:
            each_peer(lambda d: v_copy(h + 1, d, me).start())
        head = my_group * hpd + h
        kbuf[h, pl.ds(pl.multiple_of(me * tokens, tokens), tokens), :] = rk[head]
        qbuf[h, pl.ds(pl.multiple_of(me * part, part), part), :] = rq[
            head, pl.ds(pl.multiple_of(my_part * part, part), part), :
        ]

    def o_copy(h, d, s):
        head = (s // split) * hpd + h
        return pltpu.make_async_remote_copy(
            src_ref=obuf.at[h, pl.ds(pl.multiple_of(d * part, part), part)],
            dst_ref=mix.at[
                pl.ds(pl.multiple_of(lax.rem(s, split) * part, part), part),
                pl.ds(pl.multiple_of(head * dim, dim), dim),
            ],
            send_sem=osend.at[h, d],
            recv_sem=orecv.at[h, s],
            device_id={"seq": d},
            device_id_type=MESH,
        )

    block = min(256, n * part)
    in_block = block // part
    blocks = n * part // block
    factor = dim ** (-0.5) * math.log2(math.e)

    for h in range(hpd):
        own_v[h].wait()
        each_peer(lambda s: v_copy(h, s, s).wait_recv())
        each_peer(lambda s: k_copy(h, s, s).wait_recv())
        each_peer(lambda s: q_copy(h, s, s).wait_recv())

        def attend(i, carry):
            j = lax.rem(me // in_block + blocks // 2 + i, blocks)
            rows = pl.ds(pl.multiple_of(j * block, block), block)
            scores = lax.dot_general(
                qbuf[h, rows, :], kbuf[h], (((1,), (1,)), ((), ())), preferred_element_type=F32
            )
            highest = jnp.max(scores, axis=1, keepdims=True)
            exponent = jnp.exp2((scores - highest) * factor)
            total = jnp.sum(exponent, axis=1, keepdims=True)
            weights = (exponent * (1.0 / total)).astype(BF16)
            mixed = jnp.dot(weights, vbuf[h], preferred_element_type=F32)
            obuf[h, rows, :] = mixed.astype(BF16)
            for u in range(in_block):
                d = j * in_block + u

                @pl.when(d != me)
                def _():
                    o_copy(h, d, me).start()

            return carry

        lax.fori_loop(0, blocks, attend, 0, unroll=blocks <= 4)
        head = my_group * hpd + h
        mix[
            pl.ds(pl.multiple_of(my_part * part, part), part),
            pl.ds(pl.multiple_of(head * dim, dim), dim),
        ] = obuf[h, pl.ds(pl.multiple_of(me * part, part), part), :]

    load_pw.wait()
    load_cw.wait()
    for copy in later:
        copy.wait()
    for h in range(hpd):
        each_peer(lambda s: o_copy(h, s, s).wait_recv())
    features = jnp.dot(mix[...], pw[...], preferred_element_type=F32)
    center = jnp.mean(features, axis=-1, keepdims=True)
    shifted = features - center
    spread = jnp.mean(shifted * shifted, axis=-1, keepdims=True)
    act = gelu(shifted / jnp.sqrt(spread + EPSILON) * gain_ref[...]).astype(BF16)
    cols = GRID_COLS
    halo = 2 * cols
    ext[halo : halo + tokens, :] = act

    up, down = lax.rem(me + 1, n), lax.rem(me + n - 1, n)
    to_up = pltpu.make_async_remote_copy(
        src_ref=ext.at[tokens : tokens + halo],
        dst_ref=ext.at[0:halo],
        send_sem=hsend.at[0],
        recv_sem=hrecv.at[0],
        device_id={"seq": up},
        device_id_type=MESH,
    )
    to_down = pltpu.make_async_remote_copy(
        src_ref=ext.at[halo : 2 * halo],
        dst_ref=ext.at[halo + tokens : 2 * halo + tokens],
        send_sem=hsend.at[1],
        recv_sem=hrecv.at[1],
        device_id={"seq": down},
        device_id_type=MESH,
    )
    to_up.start()
    to_down.start()
    for h in range(hpd):
        each_peer(lambda d: v_copy(h, d, me).wait_send())
        each_peer(lambda d: k_copy(h, d, me).wait_send())
        each_peer(lambda d: q_copy(h, d, me).wait_send())
        each_peer(lambda d: o_copy(h, d, me).wait_send())
    to_up.wait()
    to_down.wait()

    place = lax.broadcasted_iota(jnp.int32, (tokens + 2 * halo, 1), 0)
    grid_row = place // cols + (me * strip - 2)
    inside = (grid_row >= 0) & (grid_row < strip * n)
    window = jnp.where(inside, ext[...].astype(F32), 0.0).astype(BF16)
    count = tokens + 2 * cols
    by_col = []
    for s in range(3):
        summed = None
        for r in range(3):
            term = jnp.dot(
                window[r * cols : r * cols + count], cw[3 * r + s], preferred_element_type=F32
            )
            summed = term if summed is None else summed + term
        by_col.append(summed)
    column = lax.rem(lax.broadcasted_iota(jnp.int32, (count, 1), 0), cols)
    conv = (
        by_col[1]
        + jnp.where(column == 0, 0.0, pltpu.roll(by_col[0], 1, 0))
        + jnp.where(column == cols - 1, 0.0, pltpu.roll(by_col[2], count - 1, 0))
    )
    hidden = jnp.where(inside[cols : cols + count], gelu(conv + cb_ref[...]), 0.0).astype(BF16)

    width = cols * UPSCALE
    lane = lax.broadcasted_iota(jnp.int32, (1, width), 1)
    classes = tb_ref.shape[1]
    rows_of = []
    for r in range(strip + 2):
        wide = jnp.dot(
            up_ref[...], hidden[r * cols : (r + 1) * cols], preferred_element_type=F32
        ).astype(BF16)
        taps = lax.dot_general(
            tw_ref[...], wide, (((1,), (1,)), ((), ())), preferred_element_type=F32
        )
        tap = lambda i: taps[i * classes : (i + 1) * classes]
        rows_of.append(
            [
                tap(3 * t + 1)
                + jnp.where(lane == 0, 0.0, pltpu.roll(tap(3 * t), 1, 1))
                + jnp.where(lane == width - 1, 0.0, pltpu.roll(tap(3 * t + 2), width - 1, 1))
                for t in range(3)
            ]
        )
    ids = lax.broadcasted_iota(jnp.int32, (classes, classes), 0)
    diagonal = ids == lax.broadcasted_iota(jnp.int32, (classes, classes), 1)
    bias = jnp.sum(jnp.where(diagonal, tb_ref[...], 0.0), axis=1, keepdims=True)
    ids = lax.broadcasted_iota(jnp.int32, (classes, width), 0)
    running = jnp.zeros((1, width), F32)
    for r in range(strip):
        low, here, high = rows_of[r], rows_of[r + 1], rows_of[r + 2]
        inner = here[0] + here[1] + here[2] + bias
        for phase in range(UPSCALE):
            if phase == 0:
                out = low[0] + here[1] + here[2] + bias
            elif phase == UPSCALE - 1:
                out = here[0] + here[1] + high[2] + bias
            else:
                out = inner
            y = r * UPSCALE + phase
            logits_ref[:, y, :] = out
            if phase != 2:
                highest = jnp.max(out, axis=0, keepdims=True)
                lse = highest + jnp.log(jnp.sum(jnp.exp(out - highest), axis=0, keepdims=True))
            picked = jnp.sum(
                jnp.where(ids == lab_ref[y : y + 1, :], out, 0.0), axis=0, keepdims=True
            )
            lost = lse - picked
            losses_ref[y : y + 1, :] = lost
            running = running + lost

    total = jnp.sum(running, axis=1, keepdims=True)
    part_sum[...] = jnp.broadcast_to(total, part_sum.shape)

    def l_copy(d, s):
        return pltpu.make_async_remote_copy(
            src_ref=part_sum,
            dst_ref=sums.at[s],
            send_sem=lsend.at[d],
            recv_sem=lrecv.at[s],
            device_id={"seq": d},
            device_id_type=MESH,
        )

    each_peer(lambda d: l_copy(d, me).start())
    write = [
        pltpu.make_async_copy(logits_ref, logits_out, results.at[0]),
        pltpu.make_async_copy(losses_ref, losses_out, results.at[1]),
    ]
    for copy in write:
        copy.start()
    sums[me] = part_sum[...]
    each_peer(lambda s: l_copy(s, s).wait_recv())
    each_peer(lambda d: l_copy(d, me).wait_send())
    pixels = n * strip * UPSCALE * width
    loss_ref[...] = jnp.sum(sums[...], axis=0)[0:1, 0:1] / pixels
    for copy in write:
        copy.wait()


def body(
    queries,
    keys,
    values,
    proj_weight,
    norm_gain,
    conv_weight,
    conv_bias,
    class_weight,
    class_bias,
    labels,
):
    n = lax.axis_size("seq")
    tokens = queries.shape[0]
    strip = tokens // GRID_COLS
    hpd = max(1, HEADS // n)
    split = max(1, n // HEADS)
    part = tokens // split
    channels = proj_weight.shape[1]
    classes = class_weight.shape[1]
    row_table, col_table = tables(strip * n)
    spread = np.zeros((GRID_COLS * UPSCALE, GRID_COLS), np.float32)
    spread[np.arange(GRID_COLS * UPSCALE), np.arange(GRID_COLS * UPSCALE) // UPSCALE] = 1.0
    hbm = pl.BlockSpec(memory_space=pl.ANY)
    vmem = pl.BlockSpec(memory_space=pltpu.VMEM)
    dma = pltpu.SemaphoreType.DMA
    logits, losses, loss = pl.pallas_call(
        functools.partial(kernel, n),
        out_shape=(
            jax.ShapeDtypeStruct((classes,) + labels.shape, F32),
            jax.ShapeDtypeStruct(labels.shape, F32),
            jax.ShapeDtypeStruct((1, 1), F32),
        ),
        in_specs=[hbm] * 13,
        out_specs=(hbm, hbm, vmem),
        scratch_shapes=[
            pltpu.VMEM((1, channels), F32),
            pltpu.VMEM((1, channels), F32),
            pltpu.VMEM((9 * classes, channels), BF16),
            pltpu.VMEM((1, classes), F32),
            pltpu.VMEM(labels.shape, jnp.int32),
            pltpu.VMEM(row_table.shape, F32),
            pltpu.VMEM(col_table.shape, F32),
            pltpu.VMEM(spread.shape, BF16),
            pltpu.VMEM((classes,) + labels.shape, F32),
            pltpu.VMEM(labels.shape, F32),
            pltpu.VMEM((tokens, HEADS * HEAD_DIM), BF16),
            pltpu.VMEM((tokens, HEADS * HEAD_DIM), BF16),
            pltpu.VMEM(proj_weight.shape, BF16),
            pltpu.VMEM(conv_weight.shape, BF16),
            pltpu.VMEM((HEADS, tokens, HEAD_DIM), BF16),
            pltpu.VMEM((HEADS, tokens, HEAD_DIM), BF16),
            pltpu.VMEM((hpd, n * part, HEAD_DIM), BF16),
            pltpu.VMEM((hpd, n * tokens, HEAD_DIM), BF16),
            pltpu.VMEM((hpd, n * tokens, HEAD_DIM), BF16),
            pltpu.VMEM((hpd, n * part, HEAD_DIM), BF16),
            pltpu.VMEM((tokens, HEADS * HEAD_DIM), BF16),
            pltpu.VMEM((tokens + 4 * GRID_COLS, channels), BF16),
            pltpu.VMEM((8, 128), F32),
            pltpu.VMEM((n, 8, 128), F32),
            dma((3, hpd, n)),
            dma((3, hpd, n)),
            dma((hpd, n)),
            dma((hpd, n)),
            dma((2,)),
            dma((2,)),
            dma((n,)),
            dma((n,)),
            dma((4 + hpd,)),
            dma((8,)),
            dma((2,)),
        ],
        compiler_params=pltpu.CompilerParams(
            collective_id=0, has_side_effects=True, vmem_limit_bytes=56 * 1024 * 1024
        ),
    )(
        queries,
        keys,
        values,
        proj_weight,
        norm_gain.reshape(1, -1),
        conv_weight,
        conv_bias.reshape(1, -1),
        class_weight.reshape(-1, class_weight.shape[2]),
        class_bias.reshape(1, -1),
        labels,
        jnp.asarray(row_table),
        jnp.asarray(col_table),
        jnp.asarray(spread, BF16),
    )
    return logits, losses, loss.reshape(1)


def solution(mesh):
    rows = P(("crop", "seq"), None)
    in_specs = (rows, rows, rows, P(), P(), P(), P(), P(), P(), rows)
    out_specs = (P(None, ("crop", "seq"), None), rows, P("crop"))
    return jax.shard_map(body, mesh=mesh, in_specs=in_specs, out_specs=out_specs, check_vma=False)
```

```python
import functools
import math

import jax
import jax.numpy as jnp
import numpy as np
from jax import lax
from jax.experimental import pallas as pl
from jax.experimental.pallas import tpu as pltpu
from jax.sharding import PartitionSpec as P

HEADS = 16
HEAD_DIM = 128
UPSCALE = 4
GRID_COLS = 64
EPSILON = 1e-05
MESH = pl.DeviceIdType.MESH
F32 = jnp.float32
BF16 = jnp.bfloat16


def gelu(x):
    return 0.5 * x * (1.0 + lax.erf(x * (2.0**-0.5)))


def tables(grid_rows):
    quarter = HEAD_DIM // 4
    omegas = np.power(np.float32(100.0), -np.arange(quarter, dtype=np.float32) / quarter)

    def half(count, offset):
        angles = np.arange(count, dtype=np.float32)[:, None] * omegas[None, :].astype(np.float32)
        cosine = np.cos(angles.astype(np.float64)).astype(np.float32)
        sine = np.sin(angles.astype(np.float64)).astype(np.float32)
        out = np.zeros((3, count, HEAD_DIM), np.float32)
        out[0, :, offset : offset + quarter] = cosine
        out[0, :, offset + quarter : offset + 2 * quarter] = cosine
        out[1, :, offset : offset + quarter] = -sine
        out[2, :, offset + quarter : offset + 2 * quarter] = sine
        return out

    return half(grid_rows, 0), half(GRID_COLS, 2 * quarter)


def kernel(
    n,
    q_ref,
    k_ref,
    v_ref,
    pw_ref,
    gain_in,
    cw_ref,
    cb_in,
    tw_in,
    tb_in,
    lab_in,
    row_in,
    col_in,
    up_in,
    logits_out,
    losses_out,
    loss_ref,
    gain_ref,
    cb_ref,
    tw_ref,
    tb_ref,
    lab_ref,
    row_ref,
    col_ref,
    up_ref,
    logits_ref,
    losses_ref,
    qx,
    kx,
    pw,
    cw,
    rq,
    rk,
    qbuf,
    kbuf,
    vbuf,
    obuf,
    mix,
    ext,
    part_sum,
    sums,
    ssem,
    rsem,
    osend,
    orecv,
    hsend,
    hrecv,
    lsend,
    lrecv,
    local,
    small,
    results,
):
    me = lax.axis_index("seq")
    hpd, keys, dim = kbuf.shape
    tokens = keys // n
    part = qbuf.shape[1] // n
    split = tokens // part
    strip = tokens // GRID_COLS
    my_group = me // split
    my_part = lax.rem(me, split)

    def peer(i):
        off = n // 2 + ((i + 1) // 2) * (1 - 2 * lax.rem(i, 2))
        return lax.rem(me + off, n)

    def each_peer(fn):
        def step(i, carry):
            fn(peer(i))
            return carry

        lax.fori_loop(0, n - 1, step, 0)

    def v_copy(h, d, s):
        head = (d // split) * hpd + h
        return pltpu.make_async_remote_copy(
            src_ref=v_ref.at[:, pl.ds(pl.multiple_of(head * dim, dim), dim)],
            dst_ref=vbuf.at[h, pl.ds(pl.multiple_of(s * tokens, tokens), tokens)],
            send_sem=ssem.at[0, h, d],
            recv_sem=rsem.at[0, h, s],
            device_id={"seq": d},
            device_id_type=MESH,
        )

    barrier = pltpu.get_barrier_semaphore()
    each_peer(
        lambda d: pl.semaphore_signal(barrier, inc=1, device_id={"seq": d}, device_id_type=MESH)
    )
    load_k = pltpu.make_async_copy(k_ref, kx, local.at[0])
    load_q = pltpu.make_async_copy(q_ref, qx, local.at[1])
    load_pw = [
        pltpu.make_async_copy(pw_ref.at[:, h], pw.at[h], local.at[4 + hpd + h]) for h in range(hpd)
    ]
    load_cw = pltpu.make_async_copy(cw_ref, cw, local.at[3])
    first = [
        pltpu.make_async_copy(a, b, small.at[i])
        for i, (a, b) in enumerate(((row_in, row_ref), (col_in, col_ref)))
    ]
    later = [
        pltpu.make_async_copy(a, b, small.at[i + 2])
        for i, (a, b) in enumerate(
            (
                (gain_in, gain_ref),
                (cb_in, cb_ref),
                (tw_in, tw_ref),
                (tb_in, tb_ref),
                (lab_in, lab_ref),
                (up_in, up_ref),
            )
        )
    ]
    load_k.start()
    for copy in first:
        copy.start()
    load_q.start()
    own_v = []
    for h in range(hpd):
        cols = pl.ds(pl.multiple_of((my_group * hpd + h) * dim, dim), dim)
        rows = pl.ds(pl.multiple_of(me * tokens, tokens), tokens)
        copy = pltpu.make_async_copy(v_ref.at[:, cols], vbuf.at[h, rows], local.at[4 + h])
        copy.start()
        own_v.append(copy)
    pl.semaphore_wait(barrier, n - 1)
    each_peer(lambda d: v_copy(0, d, me).start())
    for copy in load_pw:
        copy.start()
    load_cw.start()
    for copy in later:
        copy.start()
    for copy in first:
        copy.wait()

    turn = []
    for t in range(3):
        pieces = []
        for r in range(strip):
            pieces.append(row_ref[t, pl.ds(me * strip + r, 1), :] + col_ref[t])
        turn.append(jnp.concatenate(pieces, axis=0) if strip > 1 else pieces[0])

    def rotate(src, dst, h):
        for g in range(HEADS // hpd):
            head = g * hpd + h
            x = src[:, head * dim : (head + 1) * dim].astype(F32)
            out = x * turn[0] + pltpu.roll(x, 96, 1) * turn[1] + pltpu.roll(x, 32, 1) * turn[2]
            dst[head] = out.astype(BF16)

    def k_copy(h, d, s):
        return pltpu.make_async_remote_copy(
            src_ref=rk.at[(d // split) * hpd + h],
            dst_ref=kbuf.at[h, pl.ds(pl.multiple_of(s * tokens, tokens), tokens)],
            send_sem=ssem.at[1, h, d],
            recv_sem=rsem.at[1, h, s],
            device_id={"seq": d},
            device_id_type=MESH,
        )

    def q_copy(h, d, s):
        rows = pl.ds(pl.multiple_of(lax.rem(d, split) * part, part), part)
        return pltpu.make_async_remote_copy(
            src_ref=rq.at[(d // split) * hpd + h, rows],
            dst_ref=qbuf.at[h, pl.ds(pl.multiple_of(s * part, part), part)],
            send_sem=ssem.at[2, h, d],
            recv_sem=rsem.at[2, h, s],
            device_id={"seq": d},
            device_id_type=MESH,
        )

    load_k.wait()
    for h in range(hpd):
        rotate(kx, rk, h)
        each_peer(lambda d: k_copy(h, d, me).start())
        if h == 0:
            load_q.wait()
        rotate(qx, rq, h)
        each_peer(lambda d: q_copy(h, d, me).start())
        if h + 1 < hpd:
            each_peer(lambda d: v_copy(h + 1, d, me).start())
        head = my_group * hpd + h
        kbuf[h, pl.ds(pl.multiple_of(me * tokens, tokens), tokens), :] = rk[head]
        qbuf[h, pl.ds(pl.multiple_of(me * part, part), part), :] = rq[
            head, pl.ds(pl.multiple_of(my_part * part, part), part), :
        ]

    def o_copy(h, d, s):
        return pltpu.make_async_remote_copy(
            src_ref=obuf.at[h, pl.ds(pl.multiple_of(d * part, part), part)],
            dst_ref=mix.at[
                h,
                pl.ds(pl.multiple_of(lax.rem(s, split) * part, part), part),
                pl.ds(pl.multiple_of((s // split) * dim, dim), dim),
            ],
            send_sem=osend.at[h, d],
            recv_sem=orecv.at[h, s],
            device_id={"seq": d},
            device_id_type=MESH,
        )

    block = min(256, n * part)
    in_block = block // part
    blocks = n * part // block
    factor = dim ** (-0.5) * math.log2(math.e)

    for h in range(hpd):
        own_v[h].wait()
        each_peer(lambda s: v_copy(h, s, s).wait_recv())
        each_peer(lambda s: k_copy(h, s, s).wait_recv())

        def attend(i, carry):
            shift = blocks // 2 + ((i + 1) // 2) * (1 - 2 * lax.rem(i, 2))
            j = lax.rem(me // in_block + shift, blocks)
            for u in range(in_block):
                s = j * in_block + u

                @pl.when(s != me)
                def _():
                    q_copy(h, s, s).wait_recv()

            rows = pl.ds(pl.multiple_of(j * block, block), block)
            scores = lax.dot_general(
                qbuf[h, rows, :], kbuf[h], (((1,), (1,)), ((), ())), preferred_element_type=F32
            )
            highest = jnp.max(scores, axis=1, keepdims=True)
            exponent = jnp.exp2((scores - highest) * factor)
            total = jnp.sum(exponent, axis=1, keepdims=True)
            weights = (exponent * (1.0 / total)).astype(BF16)
            mixed = jnp.dot(weights, vbuf[h], preferred_element_type=F32)
            obuf[h, rows, :] = mixed.astype(BF16)
            for u in range(in_block):
                d = j * in_block + u

                @pl.when(d != me)
                def _():
                    o_copy(h, d, me).start()

            return carry

        lax.fori_loop(0, blocks, attend, 0, unroll=blocks <= 4)
        mix[
            h,
            pl.ds(pl.multiple_of(my_part * part, part), part),
            pl.ds(pl.multiple_of(my_group * dim, dim), dim),
        ] = obuf[h, pl.ds(pl.multiple_of(me * part, part), part), :]

    for copy in load_pw:
        copy.wait()
    load_cw.wait()
    for copy in later:
        copy.wait()
    features = None
    for h in range(hpd):
        each_peer(lambda s: o_copy(h, s, s).wait_recv())
        weight = pw[h].reshape(-1, pw.shape[3])
        term = jnp.dot(mix[h], weight, preferred_element_type=F32)
        features = term if features is None else features + term
    center = jnp.mean(features, axis=-1, keepdims=True)
    shifted = features - center
    spread = jnp.mean(shifted * shifted, axis=-1, keepdims=True)
    act = gelu(shifted / jnp.sqrt(spread + EPSILON) * gain_ref[...]).astype(BF16)
    cols = GRID_COLS
    halo = 2 * cols
    ext[halo : halo + tokens, :] = act

    up, down = lax.rem(me + 1, n), lax.rem(me + n - 1, n)
    to_up = pltpu.make_async_remote_copy(
        src_ref=ext.at[tokens : tokens + halo],
        dst_ref=ext.at[0:halo],
        send_sem=hsend.at[0],
        recv_sem=hrecv.at[0],
        device_id={"seq": up},
        device_id_type=MESH,
    )
    to_down = pltpu.make_async_remote_copy(
        src_ref=ext.at[halo : 2 * halo],
        dst_ref=ext.at[halo + tokens : 2 * halo + tokens],
        send_sem=hsend.at[1],
        recv_sem=hrecv.at[1],
        device_id={"seq": down},
        device_id_type=MESH,
    )

    @pl.when(me < n - 1)
    def _():
        to_up.start()

    @pl.when(me > 0)
    def _():
        to_down.start()

    for h in range(hpd):
        each_peer(lambda d: v_copy(h, d, me).wait_send())
        each_peer(lambda d: k_copy(h, d, me).wait_send())
        each_peer(lambda d: q_copy(h, d, me).wait_send())
        each_peer(lambda d: o_copy(h, d, me).wait_send())

    @pl.when(me < n - 1)
    def _():
        to_up.wait_send()
        to_down.wait_recv()

    @pl.when(me > 0)
    def _():
        to_down.wait_send()
        to_up.wait_recv()


    place = lax.broadcasted_iota(jnp.int32, (tokens + 2 * halo, 1), 0)
    grid_row = place // cols + (me * strip - 2)
    inside = (grid_row >= 0) & (grid_row < strip * n)
    window = jnp.where(inside, ext[...].astype(F32), 0.0).astype(BF16)
    count = tokens + 2 * cols
    by_col = []
    for s in range(3):
        summed = None
        for r in range(3):
            term = jnp.dot(
                window[r * cols : r * cols + count], cw[3 * r + s], preferred_element_type=F32
            )
            summed = term if summed is None else summed + term
        by_col.append(summed)
    column = lax.rem(lax.broadcasted_iota(jnp.int32, (count, 1), 0), cols)
    conv = (
        by_col[1]
        + jnp.where(column == 0, 0.0, pltpu.roll(by_col[0], 1, 0))
        + jnp.where(column == cols - 1, 0.0, pltpu.roll(by_col[2], count - 1, 0))
    )
    hidden = jnp.where(inside[cols : cols + count], gelu(conv + cb_ref[...]), 0.0).astype(BF16)

    width = cols * UPSCALE
    lane = lax.broadcasted_iota(jnp.int32, (1, width), 1)
    classes = tb_ref.shape[1]
    rows_of = []
    for r in range(strip + 2):
        wide = jnp.dot(
            up_ref[...], hidden[r * cols : (r + 1) * cols], preferred_element_type=F32
        ).astype(BF16)
        taps = lax.dot_general(
            tw_ref[...], wide, (((1,), (1,)), ((), ())), preferred_element_type=F32
        )
        tap = lambda i: taps[i * classes : (i + 1) * classes]
        rows_of.append(
            [
                tap(3 * t + 1)
                + jnp.where(lane == 0, 0.0, pltpu.roll(tap(3 * t), 1, 1))
                + jnp.where(lane == width - 1, 0.0, pltpu.roll(tap(3 * t + 2), width - 1, 1))
                for t in range(3)
            ]
        )
    ids = lax.broadcasted_iota(jnp.int32, (classes, classes), 0)
    diagonal = ids == lax.broadcasted_iota(jnp.int32, (classes, classes), 1)
    bias = jnp.sum(jnp.where(diagonal, tb_ref[...], 0.0), axis=1, keepdims=True)
    ids = lax.broadcasted_iota(jnp.int32, (classes, width), 0)
    running = jnp.zeros((1, width), F32)
    for r in range(strip):
        low, here, high = rows_of[r], rows_of[r + 1], rows_of[r + 2]
        inner = here[0] + here[1] + here[2] + bias
        for phase in range(UPSCALE):
            if phase == 0:
                out = low[0] + here[1] + here[2] + bias
            elif phase == UPSCALE - 1:
                out = here[0] + here[1] + high[2] + bias
            else:
                out = inner
            y = r * UPSCALE + phase
            logits_ref[:, y, :] = out
            if phase != 2:
                highest = jnp.max(out, axis=0, keepdims=True)
                lse = highest + jnp.log(jnp.sum(jnp.exp(out - highest), axis=0, keepdims=True))
            picked = jnp.sum(
                jnp.where(ids == lab_ref[y : y + 1, :], out, 0.0), axis=0, keepdims=True
            )
            lost = lse - picked
            losses_ref[y : y + 1, :] = lost
            running = running + lost

    total = jnp.sum(running, axis=1, keepdims=True)
    part_sum[...] = jnp.broadcast_to(total, part_sum.shape)

    def l_copy(d, s):
        return pltpu.make_async_remote_copy(
            src_ref=part_sum,
            dst_ref=sums.at[s],
            send_sem=lsend.at[d],
            recv_sem=lrecv.at[s],
            device_id={"seq": d},
            device_id_type=MESH,
        )

    each_peer(lambda d: l_copy(d, me).start())
    write = [
        pltpu.make_async_copy(logits_ref, logits_out, results.at[0]),
        pltpu.make_async_copy(losses_ref, losses_out, results.at[1]),
    ]
    for copy in write:
        copy.start()
    sums[me] = part_sum[...]
    each_peer(lambda s: l_copy(s, s).wait_recv())
    each_peer(lambda d: l_copy(d, me).wait_send())
    pixels = n * strip * UPSCALE * width
    loss_ref[...] = jnp.sum(sums[...], axis=0)[0:1, 0:1] / pixels
    for copy in write:
        copy.wait()


def body(
    queries,
    keys,
    values,
    proj_weight,
    norm_gain,
    conv_weight,
    conv_bias,
    class_weight,
    class_bias,
    labels,
):
    n = lax.axis_size("seq")
    tokens = queries.shape[0]
    strip = tokens // GRID_COLS
    hpd = max(1, HEADS // n)
    split = max(1, n // HEADS)
    part = tokens // split
    channels = proj_weight.shape[1]
    classes = class_weight.shape[1]
    row_table, col_table = tables(strip * n)
    spread = np.zeros((GRID_COLS * UPSCALE, GRID_COLS), np.float32)
    spread[np.arange(GRID_COLS * UPSCALE), np.arange(GRID_COLS * UPSCALE) // UPSCALE] = 1.0
    hbm = pl.BlockSpec(memory_space=pl.ANY)
    vmem = pl.BlockSpec(memory_space=pltpu.VMEM)
    dma = pltpu.SemaphoreType.DMA
    logits, losses, loss = pl.pallas_call(
        functools.partial(kernel, n),
        out_shape=(
            jax.ShapeDtypeStruct((classes,) + labels.shape, F32),
            jax.ShapeDtypeStruct(labels.shape, F32),
            jax.ShapeDtypeStruct((1, 1), F32),
        ),
        in_specs=[hbm] * 13,
        out_specs=(hbm, hbm, vmem),
        scratch_shapes=[
            pltpu.VMEM((1, channels), F32),
            pltpu.VMEM((1, channels), F32),
            pltpu.VMEM((9 * classes, channels), BF16),
            pltpu.VMEM((1, classes), F32),
            pltpu.VMEM(labels.shape, jnp.int32),
            pltpu.VMEM(row_table.shape, F32),
            pltpu.VMEM(col_table.shape, F32),
            pltpu.VMEM(spread.shape, BF16),
            pltpu.VMEM((classes,) + labels.shape, F32),
            pltpu.VMEM(labels.shape, F32),
            pltpu.VMEM((tokens, HEADS * HEAD_DIM), BF16),
            pltpu.VMEM((tokens, HEADS * HEAD_DIM), BF16),
            pltpu.VMEM((hpd, HEADS // hpd, HEAD_DIM, channels), BF16),
            pltpu.VMEM(conv_weight.shape, BF16),
            pltpu.VMEM((HEADS, tokens, HEAD_DIM), BF16),
            pltpu.VMEM((HEADS, tokens, HEAD_DIM), BF16),
            pltpu.VMEM((hpd, n * part, HEAD_DIM), BF16),
            pltpu.VMEM((hpd, n * tokens, HEAD_DIM), BF16),
            pltpu.VMEM((hpd, n * tokens, HEAD_DIM), BF16),
            pltpu.VMEM((hpd, n * part, HEAD_DIM), BF16),
            pltpu.VMEM((hpd, tokens, HEADS // hpd * HEAD_DIM), BF16),
            pltpu.VMEM((tokens + 4 * GRID_COLS, channels), BF16),
            pltpu.VMEM((8, 128), F32),
            pltpu.VMEM((n, 8, 128), F32),
            dma((3, hpd, n)),
            dma((3, hpd, n)),
            dma((hpd, n)),
            dma((hpd, n)),
            dma((2,)),
            dma((2,)),
            dma((n,)),
            dma((n,)),
            dma((4 + 2 * hpd,)),
            dma((8,)),
            dma((2,)),
        ],
        compiler_params=pltpu.CompilerParams(
            collective_id=0, has_side_effects=True, vmem_limit_bytes=56 * 1024 * 1024
        ),
    )(
        queries,
        keys,
        values,
        proj_weight.reshape(HEADS // hpd, hpd, HEAD_DIM, channels),
        norm_gain.reshape(1, -1),
        conv_weight,
        conv_bias.reshape(1, -1),
        class_weight.reshape(-1, class_weight.shape[2]),
        class_bias.reshape(1, -1),
        labels,
        jnp.asarray(row_table),
        jnp.asarray(col_table),
        jnp.asarray(spread, BF16),
    )
    return logits, losses, loss.reshape(1)


def solution(mesh):
    rows = P(("crop", "seq"), None)
    in_specs = (rows, rows, rows, P(), P(), P(), P(), P(), P(), rows)
    out_specs = (P(None, ("crop", "seq"), None), rows, P("crop"))
    return jax.shard_map(body, mesh=mesh, in_specs=in_specs, out_specs=out_specs, check_vma=False)
```

```python
import functools
import math

import jax
import jax.numpy as jnp
import numpy as np
from jax import lax
from jax.experimental import pallas as pl
from jax.experimental.pallas import tpu as pltpu
from jax.sharding import PartitionSpec as P

HEADS = 16
HEAD_DIM = 128
UPSCALE = 4
GRID_COLS = 64
EPSILON = 1e-05
MESH = pl.DeviceIdType.MESH
F32 = jnp.float32
BF16 = jnp.bfloat16


def gelu(x):
    return 0.5 * x * (1.0 + lax.erf(x * (2.0**-0.5)))


def tables(grid_rows):
    quarter = HEAD_DIM // 4
    omegas = np.power(np.float32(100.0), -np.arange(quarter, dtype=np.float32) / quarter)

    def half(count, offset):
        angles = np.arange(count, dtype=np.float32)[:, None] * omegas[None, :].astype(np.float32)
        cosine = np.cos(angles.astype(np.float64)).astype(np.float32)
        sine = np.sin(angles.astype(np.float64)).astype(np.float32)
        out = np.zeros((3, count, HEAD_DIM), np.float32)
        out[0, :, offset : offset + quarter] = cosine
        out[0, :, offset + quarter : offset + 2 * quarter] = cosine
        out[1, :, offset : offset + quarter] = -sine
        out[2, :, offset + quarter : offset + 2 * quarter] = sine
        return out

    return half(grid_rows, 0), half(GRID_COLS, 2 * quarter)


def kernel(
    n,
    q_ref,
    k_ref,
    v_ref,
    pw_ref,
    gain_in,
    cw_ref,
    cb_in,
    tw_in,
    tb_in,
    lab_in,
    row_in,
    col_in,
    up_in,
    logits_out,
    losses_out,
    loss_ref,
    gain_ref,
    cb_ref,
    tw_ref,
    tb_ref,
    lab_ref,
    row_ref,
    col_ref,
    up_ref,
    logits_ref,
    losses_ref,
    qx,
    kx,
    pw,
    cw,
    rq,
    rk,
    qbuf,
    kbuf,
    vbuf,
    obuf,
    mix,
    ext,
    part_sum,
    sums,
    ssem,
    rsem,
    osend,
    orecv,
    hsend,
    hrecv,
    lsend,
    lrecv,
    local,
    small,
    results,
):
    me = lax.axis_index("seq")
    hpd, keys, dim = kbuf.shape
    tokens = keys // n
    part = qbuf.shape[1] // n
    split = tokens // part
    strip = tokens // GRID_COLS
    my_group = me // split
    my_part = lax.rem(me, split)

    def peer(i):
        off = n // 2 + ((i + 1) // 2) * (1 - 2 * lax.rem(i, 2))
        return lax.rem(me + off, n)

    def each_peer(fn):
        def step(i, carry):
            fn(peer(i))
            return carry

        lax.fori_loop(0, n - 1, step, 0)

    def v_copy(h, d, s):
        head = (d // split) * hpd + h
        return pltpu.make_async_remote_copy(
            src_ref=v_ref.at[:, pl.ds(pl.multiple_of(head * dim, dim), dim)],
            dst_ref=vbuf.at[h, pl.ds(pl.multiple_of(s * tokens, tokens), tokens)],
            send_sem=ssem.at[0, h, d],
            recv_sem=rsem.at[0, h, s],
            device_id={"seq": d},
            device_id_type=MESH,
        )

    barrier = pltpu.get_barrier_semaphore()
    each_peer(
        lambda d: pl.semaphore_signal(barrier, inc=1, device_id={"seq": d}, device_id_type=MESH)
    )
    load_k = pltpu.make_async_copy(k_ref, kx, local.at[0])
    load_q = pltpu.make_async_copy(q_ref, qx, local.at[1])
    load_pw = [
        pltpu.make_async_copy(pw_ref.at[:, h], pw.at[h], local.at[4 + hpd + h]) for h in range(hpd)
    ]
    load_cw = pltpu.make_async_copy(cw_ref, cw, local.at[3])
    first = [
        pltpu.make_async_copy(a, b, small.at[i])
        for i, (a, b) in enumerate(((row_in, row_ref), (col_in, col_ref)))
    ]
    later = [
        pltpu.make_async_copy(a, b, small.at[i + 2])
        for i, (a, b) in enumerate(
            (
                (gain_in, gain_ref),
                (cb_in, cb_ref),
                (tw_in, tw_ref),
                (tb_in, tb_ref),
                (lab_in, lab_ref),
                (up_in, up_ref),
            )
        )
    ]
    load_k.start()
    for copy in first:
        copy.start()
    load_q.start()
    own_v = []
    for h in range(hpd):
        cols = pl.ds(pl.multiple_of((my_group * hpd + h) * dim, dim), dim)
        rows = pl.ds(pl.multiple_of(me * tokens, tokens), tokens)
        copy = pltpu.make_async_copy(v_ref.at[:, cols], vbuf.at[h, rows], local.at[4 + h])
        copy.start()
        own_v.append(copy)
    pl.semaphore_wait(barrier, n - 1)
    each_peer(lambda d: v_copy(0, d, me).start())
    for copy in load_pw:
        copy.start()
    load_cw.start()
    for copy in later:
        copy.start()
    for copy in first:
        copy.wait()

    turn = []
    for t in range(3):
        pieces = []
        for r in range(strip):
            pieces.append(row_ref[t, pl.ds(me * strip + r, 1), :] + col_ref[t])
        turn.append(jnp.concatenate(pieces, axis=0) if strip > 1 else pieces[0])

    def rotate(src, dst, h):
        for g in range(HEADS // hpd):
            head = g * hpd + h
            x = src[:, head * dim : (head + 1) * dim].astype(F32)
            out = x * turn[0] + pltpu.roll(x, 96, 1) * turn[1] + pltpu.roll(x, 32, 1) * turn[2]
            dst[head] = out.astype(BF16)

    def k_copy(h, d, s):
        return pltpu.make_async_remote_copy(
            src_ref=rk.at[(d // split) * hpd + h],
            dst_ref=kbuf.at[h, pl.ds(pl.multiple_of(s * tokens, tokens), tokens)],
            send_sem=ssem.at[1, h, d],
            recv_sem=rsem.at[1, h, s],
            device_id={"seq": d},
            device_id_type=MESH,
        )

    def q_copy(h, d, s):
        rows = pl.ds(pl.multiple_of(lax.rem(d, split) * part, part), part)
        return pltpu.make_async_remote_copy(
            src_ref=rq.at[(d // split) * hpd + h, rows],
            dst_ref=qbuf.at[h, pl.ds(pl.multiple_of(s * part, part), part)],
            send_sem=ssem.at[2, h, d],
            recv_sem=rsem.at[2, h, s],
            device_id={"seq": d},
            device_id_type=MESH,
        )

    load_k.wait()
    for h in range(hpd):
        rotate(kx, rk, h)
        each_peer(lambda d: k_copy(h, d, me).start())
        if h == 0:
            load_q.wait()
        rotate(qx, rq, h)
        each_peer(lambda d: q_copy(h, d, me).start())
        if h + 1 < hpd:
            each_peer(lambda d: v_copy(h + 1, d, me).start())
        head = my_group * hpd + h
        kbuf[h, pl.ds(pl.multiple_of(me * tokens, tokens), tokens), :] = rk[head]
        qbuf[h, pl.ds(pl.multiple_of(me * part, part), part), :] = rq[
            head, pl.ds(pl.multiple_of(my_part * part, part), part), :
        ]

    def o_copy(h, d, s):
        return pltpu.make_async_remote_copy(
            src_ref=obuf.at[h, pl.ds(pl.multiple_of(d * part, part), part)],
            dst_ref=mix.at[
                h,
                pl.ds(pl.multiple_of(lax.rem(s, split) * part, part), part),
                pl.ds(pl.multiple_of((s // split) * dim, dim), dim),
            ],
            send_sem=osend.at[h, d],
            recv_sem=orecv.at[h, s],
            device_id={"seq": d},
            device_id_type=MESH,
        )

    block = min(256, n * part)
    in_block = block // part
    blocks = n * part // block
    factor = dim ** (-0.5) * math.log2(math.e)

    for h in range(hpd):
        own_v[h].wait()
        each_peer(lambda s: v_copy(h, s, s).wait_recv())
        each_peer(lambda s: k_copy(h, s, s).wait_recv())

        def attend(i, carry):
            shift = blocks // 2 + ((i + 1) // 2) * (1 - 2 * lax.rem(i, 2))
            j = lax.rem(me // in_block + shift, blocks)
            for u in range(in_block):
                s = j * in_block + u

                @pl.when(s != me)
                def _():
                    q_copy(h, s, s).wait_recv()

            rows = pl.ds(pl.multiple_of(j * block, block), block)
            scores = lax.dot_general(
                qbuf[h, rows, :], kbuf[h], (((1,), (1,)), ((), ())), preferred_element_type=F32
            )
            highest = jnp.max(scores, axis=1, keepdims=True)
            exponent = jnp.exp2((scores - highest) * factor)
            total = jnp.sum(exponent, axis=1, keepdims=True)
            weights = (exponent * (1.0 / total)).astype(BF16)
            mixed = jnp.dot(weights, vbuf[h], preferred_element_type=F32)
            obuf[h, rows, :] = mixed.astype(BF16)
            for u in range(in_block):
                d = j * in_block + u

                @pl.when(d != me)
                def _():
                    o_copy(h, d, me).start()

            return carry

        lax.fori_loop(0, blocks, attend, 0, unroll=blocks <= 4)
        mix[
            h,
            pl.ds(pl.multiple_of(my_part * part, part), part),
            pl.ds(pl.multiple_of(my_group * dim, dim), dim),
        ] = obuf[h, pl.ds(pl.multiple_of(me * part, part), part), :]

    for copy in load_pw:
        copy.wait()
    load_cw.wait()
    for copy in later:
        copy.wait()
    features = None
    for h in range(hpd):
        each_peer(lambda s: o_copy(h, s, s).wait_recv())
        weight = pw[h].reshape(-1, pw.shape[3])
        term = jnp.dot(mix[h], weight, preferred_element_type=F32)
        features = term if features is None else features + term
    center = jnp.mean(features, axis=-1, keepdims=True)
    shifted = features - center
    spread = jnp.mean(shifted * shifted, axis=-1, keepdims=True)
    act = gelu(shifted / jnp.sqrt(spread + EPSILON) * gain_ref[...]).astype(BF16)
    cols = GRID_COLS
    halo = 2 * cols
    ext[halo : halo + tokens, :] = act

    up, down = lax.rem(me + 1, n), lax.rem(me + n - 1, n)
    to_up = pltpu.make_async_remote_copy(
        src_ref=ext.at[tokens : tokens + halo],
        dst_ref=ext.at[0:halo],
        send_sem=hsend.at[0],
        recv_sem=hrecv.at[0],
        device_id={"seq": up},
        device_id_type=MESH,
    )
    to_down = pltpu.make_async_remote_copy(
        src_ref=ext.at[halo : 2 * halo],
        dst_ref=ext.at[halo + tokens : 2 * halo + tokens],
        send_sem=hsend.at[1],
        recv_sem=hrecv.at[1],
        device_id={"seq": down},
        device_id_type=MESH,
    )

    @pl.when(me < n - 1)
    def _():
        to_up.start()

    @pl.when(me > 0)
    def _():
        to_down.start()

    for h in range(hpd):
        each_peer(lambda d: v_copy(h, d, me).wait_send())
        each_peer(lambda d: k_copy(h, d, me).wait_send())
        each_peer(lambda d: q_copy(h, d, me).wait_send())
        each_peer(lambda d: o_copy(h, d, me).wait_send())

    @pl.when(me < n - 1)
    def _():
        to_up.wait_send()
        to_down.wait_recv()

    @pl.when(me > 0)
    def _():
        to_down.wait_send()
        to_up.wait_recv()


    place = lax.broadcasted_iota(jnp.int32, (tokens + 2 * halo, 1), 0)
    grid_row = place // cols + (me * strip - 2)
    inside = (grid_row >= 0) & (grid_row < strip * n)
    window = jnp.where(inside, ext[...].astype(F32), 0.0).astype(BF16)
    count = tokens + 2 * cols
    by_col = []
    for s in range(3):
        summed = None
        for r in range(3):
            term = jnp.dot(
                window[r * cols : r * cols + count], cw[3 * r + s], preferred_element_type=F32
            )
            summed = term if summed is None else summed + term
        by_col.append(summed)
    column = lax.rem(lax.broadcasted_iota(jnp.int32, (count, 1), 0), cols)
    conv = (
        by_col[1]
        + jnp.where(column == 0, 0.0, pltpu.roll(by_col[0], 1, 0))
        + jnp.where(column == cols - 1, 0.0, pltpu.roll(by_col[2], count - 1, 0))
    )
    hidden = jnp.where(inside[cols : cols + count], gelu(conv + cb_ref[...]), 0.0).astype(BF16)

    width = cols * UPSCALE
    lane = lax.broadcasted_iota(jnp.int32, (1, width), 1)
    classes = tb_ref.shape[1]
    rows_of = []
    for r in range(strip + 2):
        wide = jnp.dot(
            up_ref[...], hidden[r * cols : (r + 1) * cols], preferred_element_type=F32
        ).astype(BF16)
        taps = lax.dot_general(
            tw_ref[...], wide, (((1,), (1,)), ((), ())), preferred_element_type=F32
        )
        tap = lambda i: taps[i * classes : (i + 1) * classes]
        rows_of.append(
            [
                tap(3 * t + 1)
                + jnp.where(lane == 0, 0.0, pltpu.roll(tap(3 * t), 1, 1))
                + jnp.where(lane == width - 1, 0.0, pltpu.roll(tap(3 * t + 2), width - 1, 1))
                for t in range(3)
            ]
        )
    ids = lax.broadcasted_iota(jnp.int32, (classes, classes), 0)
    diagonal = ids == lax.broadcasted_iota(jnp.int32, (classes, classes), 1)
    bias = jnp.sum(jnp.where(diagonal, tb_ref[...], 0.0), axis=1, keepdims=True)
    ids = lax.broadcasted_iota(jnp.int32, (classes, width), 0)
    running = jnp.zeros((1, width), F32)
    for r in range(strip):
        low, here, high = rows_of[r], rows_of[r + 1], rows_of[r + 2]
        inner = here[0] + here[1] + here[2] + bias
        for phase in range(UPSCALE):
            if phase == 0:
                out = low[0] + here[1] + here[2] + bias
            elif phase == UPSCALE - 1:
                out = here[0] + here[1] + high[2] + bias
            else:
                out = inner
            y = r * UPSCALE + phase
            logits_ref[:, y, :] = out
            if phase != 2:
                highest = jnp.max(out, axis=0, keepdims=True)
                lse = highest + jnp.log(jnp.sum(jnp.exp(out - highest), axis=0, keepdims=True))
            picked = jnp.sum(
                jnp.where(ids == lab_ref[y : y + 1, :], out, 0.0), axis=0, keepdims=True
            )
            lost = lse - picked
            losses_ref[y : y + 1, :] = lost
            running = running + lost

    total = jnp.sum(running, axis=1, keepdims=True)
    part_sum[...] = jnp.broadcast_to(total, part_sum.shape)

    def l_copy(d, s):
        return pltpu.make_async_remote_copy(
            src_ref=part_sum,
            dst_ref=sums.at[s],
            send_sem=lsend.at[d],
            recv_sem=lrecv.at[s],
            device_id={"seq": d},
            device_id_type=MESH,
        )

    each_peer(lambda d: l_copy(d, me).start())
    write = [
        pltpu.make_async_copy(logits_ref, logits_out, results.at[0]),
        pltpu.make_async_copy(losses_ref, losses_out, results.at[1]),
    ]
    for copy in write:
        copy.start()
    sums[me] = part_sum[...]
    each_peer(lambda s: l_copy(s, s).wait_recv())
    each_peer(lambda d: l_copy(d, me).wait_send())
    pixels = n * strip * UPSCALE * width
    loss_ref[...] = jnp.sum(sums[...], axis=0)[0:1, 0:1] / pixels
    for copy in write:
        copy.wait()


def body(
    queries,
    keys,
    values,
    proj_weight,
    norm_gain,
    conv_weight,
    conv_bias,
    class_weight,
    class_bias,
    labels,
):
    n = lax.axis_size("seq")
    tokens = queries.shape[0]
    strip = tokens // GRID_COLS
    hpd = max(1, HEADS // n)
    split = max(1, n // HEADS)
    part = tokens // split
    channels = proj_weight.shape[1]
    classes = class_weight.shape[1]
    row_table, col_table = tables(strip * n)
    spread = np.zeros((GRID_COLS * UPSCALE, GRID_COLS), np.float32)
    spread[np.arange(GRID_COLS * UPSCALE), np.arange(GRID_COLS * UPSCALE) // UPSCALE] = 1.0
    hbm = pl.BlockSpec(memory_space=pl.ANY)
    vmem = pl.BlockSpec(memory_space=pltpu.VMEM)
    dma = pltpu.SemaphoreType.DMA
    logits, losses, loss = pl.pallas_call(
        functools.partial(kernel, n),
        out_shape=(
            jax.ShapeDtypeStruct((classes,) + labels.shape, F32),
            jax.ShapeDtypeStruct(labels.shape, F32),
            jax.ShapeDtypeStruct((1, 1), F32),
        ),
        in_specs=[pl.BlockSpec(memory_space=pltpu.HBM)] * 13,
        out_specs=(hbm, hbm, vmem),
        scratch_shapes=[
            pltpu.VMEM((1, channels), F32),
            pltpu.VMEM((1, channels), F32),
            pltpu.VMEM((9 * classes, channels), BF16),
            pltpu.VMEM((1, classes), F32),
            pltpu.VMEM(labels.shape, jnp.int32),
            pltpu.VMEM(row_table.shape, F32),
            pltpu.VMEM(col_table.shape, F32),
            pltpu.VMEM(spread.shape, BF16),
            pltpu.VMEM((classes,) + labels.shape, F32),
            pltpu.VMEM(labels.shape, F32),
            pltpu.VMEM((tokens, HEADS * HEAD_DIM), BF16),
            pltpu.VMEM((tokens, HEADS * HEAD_DIM), BF16),
            pltpu.VMEM((hpd, HEADS // hpd, HEAD_DIM, channels), BF16),
            pltpu.VMEM(conv_weight.shape, BF16),
            pltpu.VMEM((HEADS, tokens, HEAD_DIM), BF16),
            pltpu.VMEM((HEADS, tokens, HEAD_DIM), BF16),
            pltpu.VMEM((hpd, n * part, HEAD_DIM), BF16),
            pltpu.VMEM((hpd, n * tokens, HEAD_DIM), BF16),
            pltpu.VMEM((hpd, n * tokens, HEAD_DIM), BF16),
            pltpu.VMEM((hpd, n * part, HEAD_DIM), BF16),
            pltpu.VMEM((hpd, tokens, HEADS // hpd * HEAD_DIM), BF16),
            pltpu.VMEM((tokens + 4 * GRID_COLS, channels), BF16),
            pltpu.VMEM((8, 128), F32),
            pltpu.VMEM((n, 8, 128), F32),
            dma((3, hpd, n)),
            dma((3, hpd, n)),
            dma((hpd, n)),
            dma((hpd, n)),
            dma((2,)),
            dma((2,)),
            dma((n,)),
            dma((n,)),
            dma((4 + 2 * hpd,)),
            dma((8,)),
            dma((2,)),
        ],
        compiler_params=pltpu.CompilerParams(
            collective_id=0, has_side_effects=True, vmem_limit_bytes=24 * 1024 * 1024
        ),
    )(
        queries,
        keys,
        values,
        proj_weight.reshape(HEADS // hpd, hpd, HEAD_DIM, channels),
        norm_gain.reshape(1, -1),
        conv_weight,
        conv_bias.reshape(1, -1),
        class_weight.reshape(-1, class_weight.shape[2]),
        class_bias.reshape(1, -1),
        labels,
        jnp.asarray(row_table),
        jnp.asarray(col_table),
        jnp.asarray(spread, BF16),
    )
    return logits, losses, loss.reshape(1)


def solution(mesh):
    rows = P(("crop", "seq"), None)
    in_specs = (rows, rows, rows, P(), P(), P(), P(), P(), P(), rows)
    out_specs = (P(None, ("crop", "seq"), None), rows, P("crop"))
    return jax.shard_map(body, mesh=mesh, in_specs=in_specs, out_specs=out_specs, check_vma=False)
```
